256 devices in a mesh: dp: 64 (over z, y, core), tensor: 4 (over x).
Axes of the slice: x: 4, y: 4, z: 8, core: 2. Of those that a mesh axis runs over, the one named last changes fastest.
Arguments:
- t_query: bfloat16 [49152, 5120], P('dp', 'tensor'), may hold values from -64 to 64
- t_key: bfloat16 [49152, 5120], P('dp', 'tensor'), may hold values from -64 to 64
- t_value: bfloat16 [49152, 5120], P('dp', 'tensor'), may hold values from -6 to 6
- t_segments: int32 [64, 768], P('dp'), may hold values from 0 to 23, never falling along the last dimension, each value on 1 to 384 neighbouring positions
- teacher_map: bfloat16 [5120, 1280], P('tensor'), may hold values from -0.625 to 0.625
- send_owner: int32 [49152], P(('dp', 'tensor')), may hold values from 0 to 63, as said below
- send_slot: int32 [49152], P(('dp', 'tensor')), may hold values from 0 to 191, as said below
- s_query: bfloat16 [49152, 1280], P(('dp', 'tensor')), may hold values from -64 to 64
- s_key: bfloat16 [49152, 1280], P(('dp', 'tensor')), may hold values from -64 to 64
- s_value: bfloat16 [49152, 1280], P(('dp', 'tensor')), may hold values from -6 to 6
- s_segments: int32 [256, 192], P(('dp', 'tensor')), may hold values from 0 to 23, never falling along the last dimension, each value on 1 to 96 neighbouring positions
- s_weight: bfloat16 [1280, 1280], P('dp'), may hold values from -0.625 to 0.625
Outputs:
- grad_context: float32 [49152, 1280], P(('dp', 'tensor'))
- grad_weight: float32 [1280, 1280], P('dp')
The draws below stay inside these ranges and needn't reach their ends.
Inputs may be any that keep to these rules, and one draw needn't show every extreme that they name: `send_owner`: the rows of one device (aligned blocks of 192 rows) send at most 6 rows to one owner, and exactly 6 to some owner. Among rows with the same t = (j // 192) % 4, the pairs (send_owner, send_slot) are all different, so each owner receives exactly 192 rows of each t.
All inputs are finite; a program needn't handle non-finite values.
Results may differ from the reference program's by a relative error of at most 0.01.
Values may be sent and summed in bfloat16 or wider, within the bound.
No kernel may reach another device: no remote copies, remote signals or barrier semaphores. Data moves between devices by JAX's collectives and lax.ppermute only.
A program may use at most 128 MiB of HBM per device.

```python
import math
import jax
import jax.numpy as jnp
import numpy as np
from jax import lax

DT = 5120
HDT = 128
DS = 1280
HDS = 64
TOKT = 768
R = 192
CAP = 6
TOKENS = 49152
N_DP = 64
N_TENSOR = 4


def aligned_pair(key, rows, width, lift, highest):
    base_query = jax.random.truncated_normal(jax.random.fold_in(key, 11), -4.0, 4.0, (rows, width), jnp.float32)
    base_key = jax.random.truncated_normal(jax.random.fold_in(key, 12), -4.0, 4.0, (rows, width), jnp.float32)
    strong = lift * jax.random.truncated_normal(jax.random.fold_in(key, 13), -4.0, 4.0, (rows, width), jnp.float32)
    strength = highest * jax.random.uniform(jax.random.fold_in(key, 14), (rows, 1), jnp.float32)
    index = jnp.arange(rows)[:, None]
    active = lift > 0.0
    marked = jnp.logical_and(index % 53 == 7, active)
    follow = jnp.logical_and(index % 53 == 8, active)
    keys = jnp.where(marked, strong, base_key)
    earlier = jnp.roll(keys, 1, axis=0)
    keys = jnp.where(follow, 0.99 * earlier, keys)
    queries = jnp.where(marked, strength * strong, base_query)
    return (queries, keys)


def route_tables(key):
    half = N_DP // 2
    order = jax.random.permutation(jax.random.fold_in(key, 102), N_DP)
    amounts = jax.random.randint(jax.random.fold_in(key, 103), (half,), 0, CAP + 1)
    amounts = jnp.where(jnp.arange(half) == 0, 0, amounts).astype(jnp.int32)
    counts = jnp.zeros((N_DP,), jnp.int32).at[order[:half]].set(CAP - amounts).at[order[half:]].set(amounts)
    senders = jnp.arange(N_DP)
    matrix = counts[(senders[None, :] - senders[:, None]) % N_DP]
    ends = jnp.cumsum(matrix, axis=1)
    firsts = ends - matrix
    column_first = jnp.cumsum(matrix, axis=0) - matrix
    position = jnp.arange(R)
    owner = jnp.sum((ends[:, None, :] <= position[None, :, None]).astype(jnp.int32), axis=2)
    owner = jnp.minimum(owner, N_DP - 1)
    place = position[None, :] - jnp.take_along_axis(firsts, owner, axis=1)
    slot_raw = jnp.take_along_axis(column_first, owner, axis=1) + place

    def one_column(column_key):
        first_key = jax.random.fold_in(column_key, 1)
        second_key = jax.random.fold_in(column_key, 2)
        shuffles = jax.vmap(lambda single: jax.random.permutation(single, R))(jax.random.split(first_key, N_DP))
        slots = shuffles[owner, slot_raw]
        reorder = jax.vmap(lambda single: jax.random.permutation(single, R))(jax.random.split(second_key, N_DP))
        inverse = jnp.argsort(reorder, axis=1)
        return (jnp.take_along_axis(owner, inverse, axis=1), jnp.take_along_axis(slots, inverse, axis=1))
    owners, slots = jax.vmap(one_column)(jax.random.split(jax.random.fold_in(key, 104), N_TENSOR))
    owners = jnp.transpose(owners, (1, 0, 2)).reshape(TOKENS).astype(jnp.int32)
    slots = jnp.transpose(slots, (1, 0, 2)).reshape(TOKENS).astype(jnp.int32)
    return (owners, slots)


def draw_send_owner(key, part):
    return route_tables(key)[0]


def draw_send_slot(key, part):
    return route_tables(key)[1]


def draw_t_query(key, part):
    lift, highest = (0.0, 0.0)
    return aligned_pair(jax.random.fold_in(key, 500), TOKENS, DT, lift, highest)[0].astype(jnp.bfloat16)


def draw_t_key(key, part):
    lift, highest = (0.0, 0.0)
    return aligned_pair(jax.random.fold_in(key, 500), TOKENS, DT, lift, highest)[1].astype(jnp.bfloat16)


def draw_s_query(key, part):
    lift, highest = (0.0, 0.0)
    return aligned_pair(jax.random.fold_in(key, 600), TOKENS, DS, lift, highest)[0].astype(jnp.bfloat16)


def draw_s_key(key, part):
    lift, highest = (0.0, 0.0)
    return aligned_pair(jax.random.fold_in(key, 600), TOKENS, DS, lift, highest)[1].astype(jnp.bfloat16)


def block_scale(key, dims, cuts, smallest, top_value):
    def one(dim, blocks):
        draws = jax.random.uniform(jax.random.fold_in(jax.random.fold_in(key, 6), dim), (blocks,), jnp.float32, smallest / len(cuts), top_value / len(cuts))
        return jnp.repeat(jnp.exp(draws), dims[dim] // blocks).reshape((-1,) + (1,) * (len(dims) - dim - 1))

    level = one(*cuts[0])
    for cut in cuts[1:]:
        level = level * one(*cut)
    return level


def split_up(number_of, total, reach, skew):
    weights = [(1 << 20) // math.isqrt(grade ** skew) + 1 for grade in range(2, number_of + 1)]
    surplus, given = total - reach - (number_of - 1), [1] * (number_of - 1)
    while surplus > 0:
        movable = [i for i in range(number_of - 1) if given[i] < reach]
        pool, remaining = sum([weights[i] for i in movable]), surplus
        for i in movable:
            more = min(reach - given[i], max(1, remaining * weights[i] // pool), surplus)
            given[i] = given[i] + more
            surplus = surplus - more
    return np.array([reach] + given)


def ragged(own_key, number_of, total, limit, lean):
    if number_of == 2:
        one = jax.random.randint(own_key, (), max(1, total - limit), min(limit, total - 1) + 1)
        return jnp.stack([one, total - one])
    lengths = jnp.asarray(split_up(number_of, total, limit, lean), jnp.int32)
    pairs = (number_of - 1) // 2
    source_of, taker = lengths[1:1 + 2 * pairs:2], lengths[2:2 + 2 * pairs:2]
    margin = jnp.minimum(source_of - 1, limit - taker)
    passed = jax.random.randint(jax.random.fold_in(own_key, 1), (pairs,), 0, 1 << 20) % (margin + 1)
    lengths = lengths.at[1:1 + 2 * pairs:2].set(source_of - passed).at[2:2 + 2 * pairs:2].set(taker + passed)
    return lengths[jax.random.permutation(jax.random.fold_in(own_key, 2), number_of)]


def scatter_about(own_key, shape, deviation, bound, cuts=(), kind=jnp.bfloat16):
    level = block_scale(own_key, shape, cuts, -0.22, 0.18) if cuts else 1.0
    result = jax.random.normal(own_key, shape, jnp.float32) * deviation * level
    return jnp.minimum(jnp.maximum(result, -bound), bound).astype(kind)


def setup_inputs(seed: int = 0) -> dict:
    seeds = jax.random.split(jax.random.key(seed), 13)
    return {
        "t_query": draw_t_query(jax.random.fold_in(seeds[12], 71), 0),
        "t_key": draw_t_key(jax.random.fold_in(seeds[12], 71), 0),
        "t_value": scatter_about(seeds[2], (TOKENS, DT), 1.0, 6.0, ((0, 64), (1, 4))),
        "t_segments": jax.vmap(lambda own: jnp.searchsorted(jnp.cumsum(ragged(own, TOKT // 32, TOKT, TOKT // 2, 2)), jnp.arange(TOKT), side="right"))(jax.random.split(seeds[3], N_DP)).reshape((N_DP, TOKT)).astype(jnp.int32),
        "teacher_map": scatter_about(seeds[4], (DT, DS), (DT // 64) ** -0.5, 0.625, ((0, 4),)),
        "send_owner": draw_send_owner(jax.random.fold_in(seeds[12], 71), 0),
        "send_slot": draw_send_slot(jax.random.fold_in(seeds[12], 71), 0),
        "s_query": draw_s_query(jax.random.fold_in(seeds[12], 71), 0),
        "s_key": draw_s_key(jax.random.fold_in(seeds[12], 71), 0),
        "s_value": scatter_about(seeds[9], (TOKENS, DS), 1.0, 6.0, ((0, 256),)),
        "s_segments": jax.vmap(lambda own: jnp.searchsorted(jnp.cumsum(ragged(own, R // 8, R, R // 2, 2)), jnp.arange(R), side="right"))(jax.random.split(seeds[10], (N_DP * N_TENSOR))).reshape((N_DP * N_TENSOR, R)).astype(jnp.int32),
        "s_weight": scatter_about(seeds[11], (DS, DS), (DS // 16) ** -0.5, 0.625, ((0, 64),)),
    }


def attend(query, keys, values, query_ids, key_ids, head_size):
    rows = query.shape[0]
    heads = query.shape[1] // head_size
    q_heads = query.astype(jnp.float32).reshape(rows, heads, head_size)
    k_heads = keys.astype(jnp.float32).reshape(-1, heads, head_size)
    v_heads = values.astype(jnp.float32).reshape(-1, heads, head_size)
    scores = jnp.einsum('qhd,khd->hqk', q_heads, k_heads) * (1.0 / math.sqrt(head_size))
    same = query_ids[:, None] == key_ids[None, :]
    scores = jnp.where(same[None], scores, jnp.float32(-1e+30))
    top = lax.optimization_barrier(jnp.max(scores, axis=2, keepdims=True))
    probs = jnp.exp(scores - top)
    weights = (probs / lax.optimization_barrier(jnp.sum(probs, axis=2, keepdims=True))).astype(jnp.bfloat16)
    mixed = jnp.einsum('hqk,khd->qhd', weights.astype(jnp.float32), v_heads)
    return mixed.reshape(rows, heads * head_size).astype(jnp.bfloat16)

def reference(t_query, t_key, t_value, t_segments, teacher_map, send_owner, send_slot, s_query, s_key, s_value, s_segments, s_weight):

    def teacher_group(pieces):
        query, keys, values, ids = pieces
        context = attend(query, keys, values, ids, ids, HDT)
        return jnp.dot(context, teacher_map, preferred_element_type=jnp.float32).astype(jnp.bfloat16)
    groups = (t_query.reshape(N_DP, TOKT, DT), t_key.reshape(N_DP, TOKT, DT), t_value.reshape(N_DP, TOKT, DT), t_segments)
    targets = lax.map(teacher_group, groups).reshape(TOKENS, DS)
    positions = jnp.arange(TOKENS, dtype=jnp.int32)
    column = positions // R % N_TENSOR
    landing = ((send_owner * N_TENSOR + column) * R + send_slot).astype(jnp.int32)
    student_target = jnp.zeros((TOKENS, DS), jnp.bfloat16).at[landing].set(targets)

    def student_block(pieces):
        query, keys, values, ids = pieces
        return attend(query, keys, values, ids, ids, HDS)
    blocks = N_DP * N_TENSOR
    student_parts = (s_query.reshape(blocks, R, DS), s_key.reshape(blocks, R, DS), s_value.reshape(blocks, R, DS), s_segments)
    context = lax.map(student_block, student_parts).reshape(TOKENS, DS)
    prediction = jnp.dot(context, s_weight, preferred_element_type=jnp.float32)
    error = (prediction - student_target.astype(jnp.float32)).astype(jnp.bfloat16)
    grad_context = jnp.dot(error, s_weight.T, preferred_element_type=jnp.float32)
    grad_weight = jnp.dot(context.T, error, preferred_element_type=jnp.float32) / math.sqrt(TOKENS)
    return (grad_context, grad_weight)
```

```python
import functools
import math

import jax
import jax.numpy as jnp
import numpy as np
from jax import lax
from jax.experimental import pallas as pl
from jax.experimental.pallas import tpu as pltpu
from jax.sharding import Mesh, PartitionSpec as P

HDT = 128
HDS = 64
LOG2E = 1.4426950408889634
BIG = 1e30
BF = jnp.bfloat16
F32 = jnp.float32
DP = ("z", "y", "core")
NT = (((1,), (1,)), ((), ()))
TN = (((0,), (0,)), ((), ()))
WIDE = 384
VMEM_LIMIT = 56 * 1024 * 1024


def ring(n, k):
    return [(i, (i + k) % n) for i in range(n)]


def params():
    return pltpu.CompilerParams(vmem_limit_bytes=VMEM_LIMIT)


def segment_columns(ids):
    n = ids.shape[1]
    lane = lax.broadcasted_iota(jnp.int32, (128, n), 0)
    hot = jnp.transpose((lane == ids).astype(F32))
    return hot.astype(BF), ((hot - 1.0) * BIG).astype(BF)


def softmax_rows(scores, scale):
    top = jnp.max(scores, axis=1, keepdims=True)
    return jnp.exp2((scores - top) * scale).astype(BF)


def teacher_kernel(x_ref, ids_ref, q_ref, k_ref, v_ref, map_ref, own_ref, right_ref, up_ref, down_ref, left_ref,
                   qx, kx, ve, ctx, packed):
    step = pl.program_id(0)
    rows = ctx.shape[0]
    half = rows // 2
    scale = LOG2E / math.sqrt(HDT)

    @pl.when(step == 0)
    def _():
        hot, far = segment_columns(ids_ref[...])
        qx[...] = hot
        kx[...] = far
        ve[:, HDT:] = jnp.ones((rows, HDT), BF)

    for h in range(2):
        cols = slice(h * HDT, (h + 1) * HDT)
        ke = jnp.concatenate([k_ref[:, cols], kx[...]], axis=1)
        ve[:, :HDT] = v_ref[:, cols]
        for r in range(0, rows, 256):
            qe = jnp.concatenate([q_ref[r:r + 256, cols], qx[r:r + 256, :]], axis=1)
            s = lax.dot_general(qe, ke, NT, preferred_element_type=F32)
            p = softmax_rows(s, scale)
            o = jnp.dot(p, ve[...], preferred_element_type=F32)
            c = (o[:, :HDT] / o[:, HDT:]).astype(BF)
            ctx[r:r + 256, pl.ds(pl.multiple_of(step * 256 + h * HDT, HDT), HDT)] = c

    @pl.when(step == pl.num_programs(0) - 1)
    def _():
        block = map_ref.shape[1] // 4
        for r in range(0, half, 192):
            a = jnp.dot(ctx[r:r + 192, :], map_ref[...], preferred_element_type=F32)
            b = jnp.dot(ctx[half + r:half + r + 192, :], map_ref[...], preferred_element_type=F32)
            for n in range(4):
                packed[n, r:r + 192, :] = jnp.concatenate(
                    [a[:, n * block:(n + 1) * block], b[:, n * block:(n + 1) * block]], axis=1
                ).astype(BF)
        x = x_ref[0]
        own_ref[...] = packed[x]
        right_ref[...] = packed[lax.rem(x + 1, 4)]
        far = lax.rem(x + 2, 4)
        up_ref[...] = packed[far, :half // 2, :]
        down_ref[...] = packed[far, half // 2:, :]
        left_ref[...] = packed[lax.rem(x + 3, 4)]


def teacher(x, ids, q, k, v, tmap):
    rows, width = q.shape
    out = tmap.shape[1]
    half = rows // 2
    wide = out // 2
    pair = 2 * HDT
    steps = width // pair
    s = lambda r: jax.ShapeDtypeStruct((r, wide), BF)
    whole = lambda r: pl.BlockSpec((r, wide), lambda i: (0, 0))
    return pl.pallas_call(
        teacher_kernel,
        grid=(steps,),
        in_specs=[
            pl.BlockSpec(memory_space=pltpu.SMEM),
            pl.BlockSpec((1, rows), lambda i: (0, 0)),
            pl.BlockSpec((rows, pair), lambda i: (0, i)),
            pl.BlockSpec((rows, pair), lambda i: (0, i)),
            pl.BlockSpec((rows, pair), lambda i: (0, i)),
            pl.BlockSpec((width, out), lambda i: (0, 0)),
        ],
        out_specs=[whole(half), whole(half), whole(half // 2), whole(half // 2), whole(half)],
        out_shape=[s(half), s(half), s(half // 2), s(half // 2), s(half)],
        scratch_shapes=[
            pltpu.VMEM((rows, 128), BF),
            pltpu.VMEM((rows, 128), BF),
            pltpu.VMEM((rows, pair), BF),
            pltpu.VMEM((rows, width), BF),
            pltpu.VMEM((4, half, wide), BF),
        ],
        compiler_params=params(),
        cost_estimate=pl.CostEstimate(flops=10 * 10**9, bytes_accessed=10 * 2**20, transcendentals=6 * 10**6),
        name="teacher",
    )(x, ids, q, k, v, tmap)


def student_kernel(ids_ref, q_ref, k_ref, v_ref, o_ref):
    rows, width = q_ref.shape
    scale = LOG2E / math.sqrt(HDS)
    hot, far = segment_columns(ids_ref[...])
    low = lax.broadcasted_iota(jnp.int32, (rows, 128), 1) < HDS
    ones = jnp.ones((rows, 128), BF)
    for g in range(0, width, 128):
        cols = slice(g, g + 128)
        ke = jnp.concatenate([k_ref[:, cols], far], axis=1)
        ve = jnp.concatenate([v_ref[:, cols], ones], axis=1)
        q = q_ref[:, cols]
        done = []
        for keep in (low, jnp.logical_not(low)):
            qe = jnp.concatenate([jnp.where(keep, q, jnp.zeros_like(q)), hot], axis=1)
            s = lax.dot_general(qe, ke, NT, preferred_element_type=F32)
            o = jnp.dot(softmax_rows(s, scale), ve, preferred_element_type=F32)
            done.append(o[:, :128] / o[:, 128:])
        o_ref[:, cols] = jnp.where(low, done[0], done[1]).astype(BF)


def student(ids, q, k, v):
    return pl.pallas_call(
        student_kernel,
        out_shape=jax.ShapeDtypeStruct(q.shape, BF),
        compiler_params=params(),
        cost_estimate=pl.CostEstimate(flops=10**9, bytes_accessed=2 * 2**20, transcendentals=10**6),
        name="student",
    )(ids, q, k, v)


def select_kernel(idx_ref, slot_ref, own_ref, a_ref, b_ref, o_ref, rows_ref):
    half, wide = own_ref.shape
    block = wide // 2
    total = (own_ref[...].astype(F32) + a_ref[...].astype(F32)) + b_ref[...].astype(F32)
    mark = jnp.transpose(jnp.broadcast_to(slot_ref[...].astype(F32) + 1.0, (128, 2 * half)))[:, :WIDE - block]
    rows_ref[:half, :] = jnp.concatenate([total[:, :block], mark[:half, :]], axis=1).astype(BF)
    rows_ref[half:, :] = jnp.concatenate([total[:, block:], mark[half:, :]], axis=1).astype(BF)
    idx = idx_ref[...]
    for r in range(0, o_ref.shape[0], 256):
        row = lax.broadcasted_iota(jnp.int32, (256, 2 * half), 0) + r
        hot = (row == idx).astype(F32).astype(BF)
        o_ref[r:r + 256, :] = jnp.dot(hot, rows_ref[...], preferred_element_type=F32).astype(BF)


def select(idx, slot, own, a, b, outgoing):
    rows = idx.shape[1]
    return pl.pallas_call(
        select_kernel,
        out_shape=jax.ShapeDtypeStruct((outgoing, WIDE), BF),
        scratch_shapes=[pltpu.VMEM((rows, WIDE), BF)],
        compiler_params=params(),
        cost_estimate=pl.CostEstimate(flops=10**9, bytes_accessed=4 * 2**20, transcendentals=0),
        name="pick",
    )(idx, slot, own, a, b)


def land_kernel(core_ref, base_ref, arrived_ref, pred_ref, ctxt_ref, err_ref, other_ref, own_ref):
    rows = err_ref.shape[0]
    block = WIDE - 64
    slot = jnp.transpose(arrived_ref[:, 256:].astype(F32))[64:65, :]
    dst = jnp.where(slot > 0.5, slot.astype(jnp.int32) + base_ref[...], -1)
    valid = lax.broadcasted_iota(jnp.int32, (256, WIDE), 1) < block
    for r in range(0, rows, 256):
        row = lax.broadcasted_iota(jnp.int32, (256, dst.shape[1]), 0) + r
        hot = (row == dst).astype(F32).astype(BF)
        target = jnp.dot(hot, arrived_ref[...], preferred_element_type=F32)
        err_ref[r:r + 256, :] = jnp.where(valid, pred_ref[r:r + 256, :] - target, 0.0).astype(BF)
    core = core_ref[0]
    other_ref[...] = jnp.dot(ctxt_ref[1 - core], err_ref[...], preferred_element_type=F32).astype(BF)
    own_ref[...] = jnp.dot(ctxt_ref[core], err_ref[...], preferred_element_type=F32)


def land(core, base, arrived, pred, ctxt):
    rows = pred.shape[0]
    out = ctxt.shape[1]
    vm = pl.BlockSpec(memory_space=pltpu.VMEM)
    return pl.pallas_call(
        land_kernel,
        in_specs=[pl.BlockSpec(memory_space=pltpu.SMEM), vm, vm, vm, vm],
        out_shape=[
            jax.ShapeDtypeStruct((rows, WIDE), BF),
            jax.ShapeDtypeStruct((out, WIDE), BF),
            jax.ShapeDtypeStruct((out, WIDE), F32),
        ],
        compiler_params=params(),
        cost_estimate=pl.CostEstimate(flops=2 * 10**9, bytes_accessed=8 * 2**20, transcendentals=0),
        name="land",
    )(core, base, arrived, pred, ctxt)


def grad_kernel(x_ref, err_ref, w_ref, own_ref, right_ref, up_ref, down_ref, left_ref):
    quarter = own_ref.shape[0]
    x = x_ref[0]

    def part(n):
        start = pl.multiple_of(lax.rem(x + n, 4) * quarter, quarter)
        return lax.dot_general(err_ref[pl.ds(start, quarter), :], w_ref[...], NT, preferred_element_type=F32)

    far = part(2).astype(BF)
    up_ref[...] = far[:quarter // 2, :]
    down_ref[...] = far[quarter // 2:, :]
    right_ref[...] = part(1).astype(BF)
    left_ref[...] = part(3).astype(BF)
    own_ref[...] = part(0)


def grad_parts(x, err, weight):
    quarter = err.shape[0] // 4
    width = weight.shape[0]
    vm = pl.BlockSpec(memory_space=pltpu.VMEM)
    s = lambda r, t=BF: jax.ShapeDtypeStruct((r, width), t)
    return pl.pallas_call(
        grad_kernel,
        in_specs=[pl.BlockSpec(memory_space=pltpu.SMEM), vm, vm],
        out_shape=[s(quarter, F32), s(quarter), s(quarter // 2), s(quarter // 2), s(quarter)],
        compiler_params=params(),
        cost_estimate=pl.CostEstimate(flops=10**9, bytes_accessed=4 * 2**20, transcendentals=0),
        name="grad",
    )(x, err, weight)


def relay_sum(right, up, down, left):
    n = up.shape[0]
    from_left = lax.ppermute(up, "tensor", ring(4, 1))
    from_right = lax.ppermute(down, "tensor", ring(4, 3))
    right = jnp.concatenate([(right[:n].astype(F32) + from_left.astype(F32)).astype(BF), right[n:]])
    left = jnp.concatenate([left[:n], (left[n:].astype(F32) + from_right.astype(F32)).astype(BF)])
    return lax.ppermute(right, "tensor", ring(4, 1)), lax.ppermute(left, "tensor", ring(4, 3))


def gather_x(a):
    x = lax.axis_index("tensor")
    parts = [a] + [lax.ppermute(a, "tensor", ring(4, k)) for k in (1, 2, 3)]
    whole = jnp.stack(parts)
    order = lax.rem(x - jnp.arange(4) + 4, 4)
    return jnp.take(whole, order, axis=0)


def local(
    t_query, t_key, t_value, t_segments, teacher_map, send_owner, send_slot, s_query, s_key, s_value, s_segments, s_weight
):
    x = lax.axis_index("tensor")
    core = lax.axis_index("core")
    rows = send_owner.shape[0]
    width = s_weight.shape[1]
    n_z, n_y, n_c = (lax.axis_size(a) for a in DP)
    owners = n_z * n_y * n_c
    capacity = 2 * rows // owners
    block = width // 4
    unit = 4 * capacity
    xs = x.astype(jnp.int32).reshape(1)
    cs = core.astype(jnp.int32).reshape(1)

    mine = lax.dynamic_slice(s_weight, (0, x * block), (s_weight.shape[0], block))
    own_rows = s_weight.shape[0]
    pad = -own_rows % 8
    mine = jnp.pad(mine, ((0, pad), (0, WIDE - block)))
    near = lax.all_to_all(
        jnp.broadcast_to(mine[None], (n_y * n_c,) + mine.shape), ("y", "core"), 0, 0, tiled=True
    ).reshape(n_y * n_c * mine.shape[0], WIDE)
    weight = lax.all_gather(near, "z", axis=0, tiled=True)
    weight = weight.reshape(owners, own_rows + pad, WIDE)[:, :own_rows].reshape(width, WIDE)

    position = jnp.arange(rows)
    same_owner = send_owner[:, None] == send_owner[None, :]
    earlier = position[:, None] > position[None, :]
    place = jnp.sum(jnp.logical_and(same_owner, earlier).astype(jnp.int32), axis=1)
    index = send_owner * unit + x * capacity + place
    table = jnp.stack([index, send_slot])
    tables = gather_x(table)
    index = tables[:, 0].reshape(1, 4 * rows)
    slots = tables[:, 1].reshape(1, 4 * rows)

    own, right, up, down, left = teacher(xs, t_segments, t_query, t_key, t_value, teacher_map)
    a, b = relay_sum(right, up, down, left)
    outgoing = select(index, slots, own, a, b, owners * unit)
    arrived = lax.all_to_all(outgoing, DP, 0, 0, tiled=True)

    context = student(s_segments, s_query, s_key, s_value)
    contexts = gather_x(context).reshape(4 * rows, width)
    prediction = jnp.dot(contexts, weight, preferred_element_type=F32)
    turned = contexts.T.reshape(n_z, n_y, n_c, own_rows, 4 * rows)
    turned = jnp.pad(jnp.transpose(turned, (2, 0, 1, 3, 4)), ((0, 0), (0, 0), (0, 0), (0, pad), (0, 0)))
    turned = turned.reshape(n_c, n_z * n_y * (own_rows + pad), 4 * rows)

    base = np.array([[(r % unit) // capacity * rows - 1 for r in range(owners * unit)]], np.int32)
    err, other, term = land(cs, jnp.asarray(base), arrived, prediction, turned)

    term = (term + lax.ppermute(other, "core", ring(2, 1)).astype(F32)).astype(BF)
    terms = lax.all_to_all(term, ("z", "y"), 0, 0, tiled=True)
    terms = terms.reshape(n_z * n_y, own_rows + pad, WIDE)[:, :own_rows, :block]
    summed = jnp.sum(terms.astype(F32), axis=0) * (1.0 / math.sqrt(4 * rows * owners))
    grad_weight = jnp.transpose(gather_x(summed), (1, 0, 2)).reshape(own_rows, width)

    own, right, up, down, left = grad_parts(xs, err, weight)
    a, b = relay_sum(right, up, down, left)
    grad_context = own + a.astype(F32) + b.astype(F32)
    return (grad_context, grad_weight)


def solution(mesh):
    fine = Mesh(mesh.devices.reshape(8, 4, 2, 4), DP + ("tensor",))
    both = DP + ("tensor",)
    placed = (
        P(DP, "tensor"),
        P(DP, "tensor"),
        P(DP, "tensor"),
        P(DP, None),
        P("tensor", None),
        P(both),
        P(both),
        P(both, None),
        P(both, None),
        P(both, None),
        P(both, None),
        P(DP, None),
    )
    return jax.shard_map(
        local, mesh=fine, in_specs=placed, out_specs=(P(both, None), P(DP, None)), check_vma=False
    )
```

```python
import functools
import math

import jax
import jax.numpy as jnp
import numpy as np
from jax import lax
from jax.experimental import pallas as pl
from jax.experimental.pallas import tpu as pltpu
from jax.sharding import Mesh, PartitionSpec as P

HDT = 128
HDS = 64
LOG2E = 1.4426950408889634
BIG = 1e30
BF = jnp.bfloat16
F32 = jnp.float32
DP = ("z", "y", "core")
NT = (((1,), (1,)), ((), ()))
TN = (((0,), (0,)), ((), ()))
WIDE = 384
TABLE = 16
MIB = 1024 * 1024


def ring(n, k):
    return [(i, (i + k) % n) for i in range(n)]


def params(mib):
    return pltpu.CompilerParams(vmem_limit_bytes=mib * MIB)


def segment_columns(ids):
    n = ids.shape[1]
    lane = lax.broadcasted_iota(jnp.int32, (128, n), 0)
    hot = jnp.transpose((lane == ids).astype(F32))
    return hot.astype(BF), ((hot - 1.0) * BIG).astype(BF)


def softmax_rows(scores, scale):
    top = jnp.max(scores, axis=1, keepdims=True)
    return jnp.exp2((scores - top) * scale).astype(BF)


def send_table(owner, slot, wide):
    n = owner.shape[1]
    across = owner.astype(F32)
    down = jnp.transpose(jnp.broadcast_to(across, (128, n)))[:, 0:1]
    before = lax.broadcasted_iota(jnp.int32, (n, n), 0) < lax.broadcasted_iota(jnp.int32, (n, n), 1)
    place = jnp.sum(jnp.where(jnp.logical_and(down == across, before), 1.0, 0.0), axis=0, keepdims=True)
    row = lax.broadcasted_iota(jnp.int32, (TABLE, n), 0)
    table = jnp.where(row == 0, across, jnp.where(row == 1, place, jnp.where(row == 2, slot.astype(F32), 0.0)))
    return jnp.concatenate([table, jnp.zeros((TABLE, wide - n), F32)], axis=1).astype(BF)


def teacher_kernel(x_ref, ids_ref, sends_ref, w_ref, q_ref, k_ref, v_ref, map_hbm, out_ref, mine_ref, qx, kx, ve, ctx,
                   map_ref, sem):
    step = pl.program_id(0)
    fetch = pltpu.make_async_copy(map_hbm, map_ref, sem)
    rows = ctx.shape[0]
    half = rows // 2
    scale = LOG2E / math.sqrt(HDT)

    @pl.when(step == 0)
    def _():
        fetch.start()
        hot, far = segment_columns(ids_ref[...])
        qx[...] = hot
        kx[...] = far
        ve[:, HDT:] = jnp.ones((rows, HDT), BF)
        table = send_table(sends_ref[0:1, :], sends_ref[1:2, :], out_ref.shape[2])
        for n in range(4):
            out_ref[n, half:, :] = table
        weight = w_ref[...].astype(F32)
        block = weight.shape[1] // 4
        rest = jnp.zeros((weight.shape[0], WIDE - block), F32)
        below = jnp.zeros((mine_ref.shape[0] - weight.shape[0], WIDE), F32)
        for n in range(4):
            @pl.when(x_ref[0] == n)
            def _():
                part = jnp.concatenate([weight[:, n * block:(n + 1) * block], rest], axis=1)
                mine_ref[...] = jnp.concatenate([part, below], axis=0).astype(BF)

    for h in range(2):
        cols = slice(h * HDT, (h + 1) * HDT)
        ke = jnp.concatenate([k_ref[:, cols], kx[...]], axis=1)
        ve[:, :HDT] = v_ref[:, cols]
        for r in range(0, rows, 256):
            qe = jnp.concatenate([q_ref[r:r + 256, cols], qx[r:r + 256, :]], axis=1)
            s = lax.dot_general(qe, ke, NT, preferred_element_type=F32)
            p = softmax_rows(s, scale)
            o = jnp.dot(p, ve[...], preferred_element_type=F32)
            c = (o[:, :HDT] / o[:, HDT:]).astype(BF)
            ctx[r:r + 256, pl.ds(pl.multiple_of(step * 256 + h * HDT, HDT), HDT)] = c

    @pl.when(step == pl.num_programs(0) - 1)
    def _():
        fetch.wait()
        block = map_ref.shape[1] // 4
        for r in range(0, half, 192):
            a = jnp.dot(ctx[r:r + 192, :], map_ref[...], preferred_element_type=F32)
            b = jnp.dot(ctx[half + r:half + r + 192, :], map_ref[...], preferred_element_type=F32)
            for n in range(4):
                out_ref[n, r:r + 192, :] = jnp.concatenate(
                    [a[:, n * block:(n + 1) * block], b[:, n * block:(n + 1) * block]], axis=1
                ).astype(BF)


def teacher(x, ids, sends, weight, q, k, v, tmap):
    rows, width = q.shape
    out = tmap.shape[1]
    half = rows // 2
    wide = out // 2
    pair = 2 * HDT
    steps = width // pair
    shapes = [(4, half + TABLE, wide), (weight.shape[0] + -weight.shape[0] % 8, WIDE)]
    return pl.pallas_call(
        teacher_kernel,
        grid=(steps,),
        in_specs=[
            pl.BlockSpec(memory_space=pltpu.SMEM),
            pl.BlockSpec((1, rows), lambda i: (0, 0)),
            pl.BlockSpec(sends.shape, lambda i: (0, 0)),
            pl.BlockSpec(weight.shape, lambda i: (0, 0)),
            pl.BlockSpec((rows, pair), lambda i: (0, i)),
            pl.BlockSpec((rows, pair), lambda i: (0, i)),
            pl.BlockSpec((rows, pair), lambda i: (0, i)),
            pl.BlockSpec(memory_space=pl.ANY),
        ],
        out_specs=[pl.BlockSpec(shapes[0], lambda i: (0, 0, 0)), pl.BlockSpec(shapes[1], lambda i: (0, 0))],
        out_shape=[jax.ShapeDtypeStruct(shape, BF) for shape in shapes],
        scratch_shapes=[
            pltpu.VMEM((rows, 128), BF),
            pltpu.VMEM((rows, 128), BF),
            pltpu.VMEM((rows, pair), BF),
            pltpu.VMEM((rows, width), BF),
            pltpu.VMEM((width, out), BF),
            pltpu.SemaphoreType.DMA,
        ],
        compiler_params=params(60),
        cost_estimate=pl.CostEstimate(flops=10 * 10**9, bytes_accessed=10 * 2**20, transcendentals=6 * 10**6),
        name="teacher",
    )(x, ids, sends, weight, q, k, v, tmap)


def student_kernel(ids_ref, q_ref, k_ref, v_ref, o_ref):
    rows, width = q_ref.shape
    scale = LOG2E / math.sqrt(HDS)
    hot, far = segment_columns(ids_ref[...])
    low = lax.broadcasted_iota(jnp.int32, (rows, 128), 1) < HDS
    ones = jnp.ones((rows, 128), BF)
    for g in range(0, width, 128):
        cols = slice(g, g + 128)
        ke = jnp.concatenate([k_ref[:, cols], far], axis=1)
        ve = jnp.concatenate([v_ref[:, cols], ones], axis=1)
        q = q_ref[:, cols]
        done = []
        for keep in (low, jnp.logical_not(low)):
            qe = jnp.concatenate([jnp.where(keep, q, jnp.zeros_like(q)), hot], axis=1)
            s = lax.dot_general(qe, ke, NT, preferred_element_type=F32)
            o = jnp.dot(softmax_rows(s, scale), ve, preferred_element_type=F32)
            done.append(o[:, :128] / o[:, 128:])
        o_ref[:, cols] = jnp.where(low, done[0], done[1]).astype(BF)


def student(ids, q, k, v):
    return pl.pallas_call(
        student_kernel,
        out_shape=jax.ShapeDtypeStruct(q.shape, BF),
        compiler_params=params(24),
        cost_estimate=pl.CostEstimate(flops=10**9, bytes_accessed=2 * 2**20, transcendentals=10**6),
        name="student",
    )(ids, q, k, v)


def select_kernel(capacity, unit, parts_ref, o_ref, rows_ref):
    half = parts_ref.shape[1] - TABLE
    block = parts_ref.shape[2] // 2
    quarter = half // 2
    table = [parts_ref[n, half:, :quarter].astype(F32) for n in range(4)]
    idx = jnp.concatenate(
        [t[0:1, :] * unit + t[1:2, :] + n * capacity for n, t in enumerate(table)], axis=1
    ).astype(jnp.int32)
    slot = jnp.concatenate([t[2:3, :] for t in table], axis=1)
    mark = jnp.transpose(jnp.broadcast_to(slot + 1.0, (128, 2 * half)))[:, :WIDE - block]
    for r in (0, quarter):
        a, b, c, d = (parts_ref[n, r:r + quarter, :].astype(F32) for n in range(4))
        total = (a + b) + (c + d)
        for c, m in ((0, r), (block, half + r)):
            rows_ref[m:m + quarter, :] = jnp.concatenate(
                [total[:, c:c + block], mark[m:m + quarter, :]], axis=1
            ).astype(BF)
    for r in range(0, o_ref.shape[0], 256):
        row = lax.broadcasted_iota(jnp.int32, (256, 2 * half), 0) + r
        hot = (row == idx).astype(F32).astype(BF)
        o_ref[r:r + 256, :] = jnp.dot(hot, rows_ref[...], preferred_element_type=F32).astype(BF)


def select(parts, owners, capacity):
    unit = 4 * capacity
    return pl.pallas_call(
        functools.partial(select_kernel, capacity, unit),
        out_shape=jax.ShapeDtypeStruct((owners * unit, WIDE), BF),
        scratch_shapes=[pltpu.VMEM((2 * (parts.shape[1] - TABLE), WIDE), BF)],
        compiler_params=params(16),
        cost_estimate=pl.CostEstimate(flops=10**9, bytes_accessed=4 * 2**20, transcendentals=0),
        name="pick",
    )(parts)


def project_kernel(unit, padded, at_ref, c0_ref, c1_ref, c2_ref, c3_ref, c4_ref, near_ref, other_ref, pred_ref, ctxt_ref, w_ref, ctx,
                   raw, rows):
    count = near_ref.shape[0] // padded
    raw[:count] = near_ref[...].astype(F32).reshape(count, padded, WIDE)
    raw[count:] = other_ref[...].astype(F32).reshape(count, padded, WIDE)
    z, y, c = at_ref[0], at_ref[1], at_ref[2]
    row = 0
    for m in range(8):
        d = lax.rem(z - m + 8, 8)
        turn = (d % 2) * 4 + d // 2
        for n in range(4):
            for o in range(2):
                at = lax.rem(c + o, 2) * count + lax.rem(y - n + 4, 4) * 8 + turn
                rows[row:row + unit, :] = raw[at, :unit, :]
                row += unit
    w_ref[...] = rows[...].astype(BF)
    start = 0
    for c_ref in (c0_ref, c1_ref, c2_ref, c3_ref, c4_ref):
        ctx[start:start + c_ref.shape[0], :] = c_ref[...]
        start += c_ref.shape[0]
    for c in range(0, ctx.shape[1], 256):
        for r in range(0, ctx.shape[0], 256):
            ctxt_ref[c:c + 256, r:r + 256] = jnp.transpose(ctx[r:r + 256, c:c + 256].astype(F32)).astype(BF)
    pred_ref[...] = jnp.dot(ctx[...], w_ref[...], preferred_element_type=F32)


def project(at, pieces, near, other, unit, padded):
    quarter, width = pieces[0].shape
    vm = pl.BlockSpec(memory_space=pltpu.VMEM)
    return pl.pallas_call(
        functools.partial(project_kernel, unit, padded),
        in_specs=[pl.BlockSpec(memory_space=pltpu.SMEM)] + [vm] * 7,
        out_shape=[
            jax.ShapeDtypeStruct((4 * quarter, WIDE), F32),
            jax.ShapeDtypeStruct((width, 4 * quarter), BF),
            jax.ShapeDtypeStruct((width, WIDE), BF),
        ],
        scratch_shapes=[
            pltpu.VMEM((4 * quarter, width), BF),
            pltpu.VMEM((width // unit, padded, WIDE), F32),
            pltpu.VMEM((width, WIDE), F32),
        ],
        compiler_params=params(60),
        cost_estimate=pl.CostEstimate(flops=10**9, bytes_accessed=8 * 2**20, transcendentals=0),
        name="project",
    )(at, *pieces, near, other)


def land_kernel(unit, place_ref, t_ref, arrived_ref, pred_ref, ctxt_ref, err_ref, other_ref, own_ref, blocks):
    rows = err_ref.shape[0]
    quarter = rows // 4
    block = WIDE - 64
    slot = jnp.transpose(arrived_ref[:, 256:].astype(F32))[64:65, :].astype(jnp.int32)
    base = jnp.bitwise_and(place_ref[0] + 4 - t_ref[...], 3) * quarter - 1
    dst = jnp.where(slot > 0, slot + base, -1)
    valid = lax.broadcasted_iota(jnp.int32, (256, WIDE), 1) < block
    for r in range(0, rows, 256):
        row = lax.broadcasted_iota(jnp.int32, (256, dst.shape[1]), 0) + r
        hot = (row == dst).astype(F32).astype(BF)
        target = jnp.dot(hot, arrived_ref[...], preferred_element_type=F32)
        err_ref[r:r + 256, :] = jnp.where(valid, pred_ref[r:r + 256, :] - target, 0.0).astype(BF)
    n = ctxt_ref.shape[0] // (2 * unit)
    chunk = 4 * 2 * unit
    blocks[...] = jnp.zeros_like(blocks)
    for i in range(0, 2 * n, 8):
        term = jnp.dot(ctxt_ref[i * unit:i * unit + chunk, :], err_ref[...], preferred_element_type=F32)
        for j in range(8):
            blocks[j % 2, (i + j) // 2, :unit, :] = term[j * unit:(j + 1) * unit, :]
    core = place_ref[1]
    other_ref[...] = blocks[1 - core].reshape(other_ref.shape).astype(BF)
    own_ref[...] = blocks[core].reshape(own_ref.shape)


def land(place, kinds, arrived, pred, ctxt, unit, padded):
    rows = pred.shape[0]
    n = ctxt.shape[0] // (2 * unit)
    vm = pl.BlockSpec(memory_space=pltpu.VMEM)
    return pl.pallas_call(
        functools.partial(land_kernel, unit),
        in_specs=[pl.BlockSpec(memory_space=pltpu.SMEM), vm, vm, vm, vm],
        out_shape=[
            jax.ShapeDtypeStruct((rows, WIDE), BF),
            jax.ShapeDtypeStruct((n * padded, WIDE), BF),
            jax.ShapeDtypeStruct((n * padded, WIDE), F32),
        ],
        scratch_shapes=[pltpu.VMEM((2, n, padded, WIDE), F32)],
        compiler_params=params(24),
        cost_estimate=pl.CostEstimate(flops=2 * 10**9, bytes_accessed=8 * 2**20, transcendentals=0),
        name="land",
    )(place, kinds, arrived, pred, ctxt)


def grad_kernel(err_ref, w_ref, own_ref, left_ref, far_ref, right_ref):
    quarter = own_ref.shape[0]
    for k, ref in enumerate((own_ref, left_ref, far_ref, right_ref)):
        part = lax.dot_general(err_ref[k * quarter:(k + 1) * quarter, :], w_ref[...], NT, preferred_element_type=F32)
        ref[...] = part.astype(ref.dtype)


def grad_parts(err, weight):
    quarter = err.shape[0] // 4
    width = weight.shape[0]
    return pl.pallas_call(
        grad_kernel,
        out_shape=[jax.ShapeDtypeStruct((quarter, width), t) for t in (F32, BF, BF, BF)],
        compiler_params=params(16),
        cost_estimate=pl.CostEstimate(flops=10**9, bytes_accessed=4 * 2**20, transcendentals=0),
        name="grad",
    )(err, weight)


def after(value, *earlier):
    return lax.optimization_barrier((value,) + earlier)[0]


def go(a, k, axis="tensor"):
    return lax.ppermute(a, axis, ring(lax.axis_size(axis), k))


def add(a, b):
    return (a.astype(F32) + b.astype(F32)).astype(BF)


def pieces_x(a):
    return [a] + [go(a, k) for k in (1, 2, 3)]


def local(
    t_query, t_key, t_value, t_segments, teacher_map, send_owner, send_slot, s_query, s_key, s_value, s_segments, s_weight
):
    x = lax.axis_index("tensor")
    core = lax.axis_index("core")
    rows = send_owner.shape[0]
    width = s_weight.shape[1]
    n_z, n_y, n_c = (lax.axis_size(a) for a in DP)
    owners = n_z * n_y * n_c
    capacity = 2 * rows // owners
    block = width // 4
    unit = 4 * capacity
    place2 = jnp.stack([x, core]).astype(jnp.int32)
    xs = x.astype(jnp.int32).reshape(1)
    own_rows = s_weight.shape[0]
    padded = own_rows + -own_rows % 8

    sends = jnp.stack([send_owner, send_slot])
    parts, mine = teacher(xs, t_segments, sends, s_weight, t_query, t_key, t_value, teacher_map)
    parts = lax.all_to_all(parts, "tensor", 0, 0, tiled=True)
    outgoing = select(parts, owners, capacity)

    far = jnp.concatenate([mine] + [go(mine, k, "z") for k in (2, 4, 6)])
    far = jnp.concatenate([far, go(far, 1, "z")])
    first = go(far, 1, "y")
    last = go(far, 3, "y")
    context = student(s_segments, s_query, s_key, after(s_value, mine))

    outgoing, far, first, last, context = lax.optimization_barrier((outgoing, far, first, last, context))
    arrived = lax.all_to_all(outgoing, DP, 0, 0, tiled=True)

    right = go(context, 1)
    left = go(context, 3)
    contexts = (context, right, go(right[:rows // 2], 1), go(left[rows // 2:], 3), left)
    half = far.shape[0] // 2
    near = jnp.concatenate([far, first, go(first[:half], 1, "y"), go(last[half:], 3, "y"), last])
    where = jnp.stack([lax.axis_index(a) for a in DP]).astype(jnp.int32)
    prediction, turned, weight = project(where, contexts, near, go(near, 1, "core"), own_rows, padded)

    kinds = np.array([[(r % unit) // capacity for r in range(owners * unit)]], np.int32)
    err, other, term = land(place2, jnp.asarray(kinds), arrived, prediction, turned, own_rows, padded)
    own, *parts = grad_parts(err, weight)

    other, parts = lax.optimization_barrier((go(other, 1, "core"), parts))
    term = add(term, other)
    terms = lax.all_to_all(term, ("z", "y"), 0, 0, tiled=True)
    terms = terms.reshape(n_z * n_y, padded, WIDE)[:, :own_rows, :block]
    summed = jnp.sum(terms.astype(F32), axis=0) * (1.0 / math.sqrt(4 * rows * owners))
    whole = jnp.stack(pieces_x(summed))
    order = lax.rem(x - jnp.arange(4) + 4, 4)
    grad_weight = jnp.transpose(jnp.take(whole, order, axis=0), (1, 0, 2)).reshape(own_rows, width)

    grad_context = own + sum(go(part, 4 - k).astype(F32) for k, part in enumerate(parts, 1))
    return (grad_context, grad_weight)


def solution(mesh):
    fine = Mesh(mesh.devices.reshape(8, 4, 2, 4), DP + ("tensor",))
    both = DP + ("tensor",)
    placed = (
        P(DP, "tensor"),
        P(DP, "tensor"),
        P(DP, "tensor"),
        P(DP, None),
        P("tensor", None),
        P(both),
        P(both),
        P(both, None),
        P(both, None),
        P(both, None),
        P(both, None),
        P(DP, None),
    )
    return jax.shard_map(
        local, mesh=fine, in_specs=placed, out_specs=(P(both, None), P(DP, None)), check_vma=False
    )
```

```python
import functools
import math

import jax
import jax.numpy as jnp
import numpy as np
from jax import lax
from jax.experimental import pallas as pl
from jax.experimental.pallas import tpu as pltpu
from jax.sharding import Mesh, PartitionSpec as P

HDT = 128
HDS = 64
LOG2E = 1.4426950408889634
BIG = 1e30
BF = jnp.bfloat16
F32 = jnp.float32
DP = ("z", "y", "core")
NT = (((1,), (1,)), ((), ()))
TN = (((0,), (0,)), ((), ()))
WIDE = 384
TABLE = 16
MIB = 1024 * 1024


def ring(n, k):
    return [(i, (i + k) % n) for i in range(n)]


def params(mib):
    return pltpu.CompilerParams(vmem_limit_bytes=mib * MIB)


def segment_columns(ids):
    n = ids.shape[1]
    lane = lax.broadcasted_iota(jnp.int32, (128, n), 0)
    hot = jnp.transpose((lane == ids).astype(F32))
    return hot.astype(BF), ((hot - 1.0) * BIG).astype(BF)


def softmax_rows(scores, scale):
    top = jnp.max(scores, axis=1, keepdims=True)
    return jnp.exp2((scores - top) * scale).astype(BF)


def send_table(owner, slot, wide):
    n = owner.shape[1]
    across = owner.astype(F32)
    down = jnp.transpose(jnp.broadcast_to(across, (128, n)))[:, 0:1]
    before = lax.broadcasted_iota(jnp.int32, (n, n), 0) < lax.broadcasted_iota(jnp.int32, (n, n), 1)
    place = jnp.sum(jnp.where(jnp.logical_and(down == across, before), 1.0, 0.0), axis=0, keepdims=True)
    row = lax.broadcasted_iota(jnp.int32, (TABLE, n), 0)
    table = jnp.where(row == 0, across, jnp.where(row == 1, place, jnp.where(row == 2, slot.astype(F32), 0.0)))
    return jnp.concatenate([table, jnp.zeros((TABLE, wide - n), F32)], axis=1).astype(BF)


def teacher_kernel(x_ref, ids_ref, owner_ref, slot_ref, w_ref, q_ref, k_ref, v_ref, map_hbm, out_ref, mine_ref, qx, kx, ve, ctx,
                   map_ref, sem):
    step = pl.program_id(0)
    fetch = pltpu.make_async_copy(map_hbm, map_ref, sem)
    rows = ctx.shape[0]
    half = rows // 2
    scale = LOG2E / math.sqrt(HDT)

    @pl.when(step == 0)
    def _():
        fetch.start()
        hot, far = segment_columns(ids_ref[...])
        qx[...] = hot
        kx[...] = far
        ve[:, :, HDT:] = jnp.ones((2, rows, HDT), BF)
        table = send_table(owner_ref[...].reshape(1, -1), slot_ref[...].reshape(1, -1), out_ref.shape[2])
        for n in range(4):
            out_ref[n, half:, :] = table
        weight = w_ref[...].astype(F32)
        block = weight.shape[1] // 4
        rest = jnp.zeros((weight.shape[0], WIDE - block), F32)
        below = jnp.zeros((mine_ref.shape[0] - weight.shape[0], WIDE), F32)
        for n in range(4):
            @pl.when(x_ref[0] == n)
            def _():
                part = jnp.concatenate([weight[:, n * block:(n + 1) * block], rest], axis=1)
                mine_ref[...] = jnp.concatenate([part, below], axis=0).astype(BF)

    for h in range(2):
        cols = slice(h * HDT, (h + 1) * HDT)
        ke = jnp.concatenate([k_ref[:, cols], kx[...]], axis=1)
        ve[h, :, :HDT] = v_ref[:, cols]
        for r in range(0, rows, 256):
            qe = jnp.concatenate([q_ref[r:r + 256, cols], qx[r:r + 256, :]], axis=1)
            s = lax.dot_general(qe, ke, NT, preferred_element_type=F32)
            p = softmax_rows(s, scale)
            o = jnp.dot(p, ve[h], preferred_element_type=F32)
            c = (o[:, :HDT] / o[:, HDT:]).astype(BF)
            ctx[r:r + 256, pl.ds(pl.multiple_of(step * 256 + h * HDT, HDT), HDT)] = c

    @pl.when(step == pl.num_programs(0) - 1)
    def _():
        fetch.wait()
        block = map_ref.shape[1] // 4
        for r in range(0, half, 192):
            a = jnp.dot(ctx[r:r + 192, :], map_ref[...], preferred_element_type=F32)
            b = jnp.dot(ctx[half + r:half + r + 192, :], map_ref[...], preferred_element_type=F32)
            for n in range(4):
                out_ref[n, r:r + 192, :] = jnp.concatenate(
                    [a[:, n * block:(n + 1) * block], b[:, n * block:(n + 1) * block]], axis=1
                ).astype(BF)


def teacher(x, ids, owner, slot, weight, q, k, v, tmap):
    rows, width = q.shape
    out = tmap.shape[1]
    half = rows // 2
    wide = out // 2
    pair = 2 * HDT
    steps = width // pair
    shapes = [(4, half + TABLE, wide), (weight.shape[0] + -weight.shape[0] % 8, WIDE)]
    return pl.pallas_call(
        teacher_kernel,
        grid=(steps,),
        in_specs=[
            pl.BlockSpec(memory_space=pltpu.SMEM),
            pl.BlockSpec((1, rows), lambda i: (0, 0)),
            pl.BlockSpec(owner.shape, lambda i: (0,)),
            pl.BlockSpec(slot.shape, lambda i: (0,)),
            pl.BlockSpec(weight.shape, lambda i: (0, 0)),
            pl.BlockSpec((rows, pair), lambda i: (0, i)),
            pl.BlockSpec((rows, pair), lambda i: (0, i)),
            pl.BlockSpec((rows, pair), lambda i: (0, i)),
            pl.BlockSpec(memory_space=pl.ANY),
        ],
        out_specs=[pl.BlockSpec(shapes[0], lambda i: (0, 0, 0)), pl.BlockSpec(shapes[1], lambda i: (0, 0))],
        out_shape=[jax.ShapeDtypeStruct(shape, BF) for shape in shapes],
        scratch_shapes=[
            pltpu.VMEM((rows, 128), BF),
            pltpu.VMEM((rows, 128), BF),
            pltpu.VMEM((2, rows, pair), BF),
            pltpu.VMEM((rows, width), BF),
            pltpu.VMEM((width, out), BF),
            pltpu.SemaphoreType.DMA,
        ],
        compiler_params=params(60),
        cost_estimate=pl.CostEstimate(flops=10 * 10**9, bytes_accessed=10 * 2**20, transcendentals=6 * 10**6),
        name="teacher",
    )(x, ids, owner, slot, weight, q, k, v, tmap)


def student_kernel(ids_ref, q_ref, k_ref, v_ref, o_ref):
    rows, width = q_ref.shape
    scale = LOG2E / math.sqrt(HDS)
    hot, far = segment_columns(ids_ref[...])
    low = lax.broadcasted_iota(jnp.int32, (rows, 128), 1) < HDS
    ones = jnp.ones((rows, 128), BF)
    for g in range(0, width, 128):
        cols = slice(g, g + 128)
        ke = jnp.concatenate([k_ref[:, cols], far], axis=1)
        ve = jnp.concatenate([v_ref[:, cols], ones], axis=1)
        q = q_ref[:, cols]
        done = []
        for keep in (low, jnp.logical_not(low)):
            qe = jnp.concatenate([jnp.where(keep, q, jnp.zeros_like(q)), hot], axis=1)
            s = lax.dot_general(qe, ke, NT, preferred_element_type=F32)
            o = jnp.dot(softmax_rows(s, scale), ve, preferred_element_type=F32)
            done.append(o[:, :128] / o[:, 128:])
        o_ref[:, cols] = jnp.where(low, done[0], done[1]).astype(BF)


def student(ids, q, k, v):
    return pl.pallas_call(
        student_kernel,
        out_shape=jax.ShapeDtypeStruct(q.shape, BF),
        compiler_params=params(24),
        cost_estimate=pl.CostEstimate(flops=10**9, bytes_accessed=2 * 2**20, transcendentals=10**6),
        name="student",
    )(ids, q, k, v)


def one_hot(row, index, start):
    near = jnp.minimum(jnp.maximum(index - start, -1.0), 256.0).astype(BF)
    return jnp.where(row == near, jnp.ones_like(row), jnp.zeros_like(row))


def count_rows(n):
    return lax.broadcasted_iota(jnp.int32, (256, n), 0).astype(F32).astype(BF)


def select_kernel(capacity, unit, parts_ref, o_ref, rows_ref):
    half = parts_ref.shape[1] - TABLE
    block = parts_ref.shape[2] // 2
    quarter = half // 2
    table = [parts_ref[n, half:, :quarter].astype(F32) for n in range(4)]
    idx = jnp.concatenate(
        [t[0:1, :] * unit + t[1:2, :] + n * capacity for n, t in enumerate(table)], axis=1
    )
    slot = jnp.concatenate([t[2:3, :] for t in table], axis=1)
    mark = jnp.transpose(jnp.broadcast_to(slot + 1.0, (128, 2 * half)))[:, :WIDE - block]
    for r in (0, quarter):
        a, b, c, d = (parts_ref[n, r:r + quarter, :].astype(F32) for n in range(4))
        total = (a + b) + (c + d)
        for c, m in ((0, r), (block, half + r)):
            rows_ref[m:m + quarter, :] = jnp.concatenate(
                [total[:, c:c + block], mark[m:m + quarter, :]], axis=1
            ).astype(BF)
    row = count_rows(2 * half)
    for r in range(0, o_ref.shape[0], 256):
        hot = one_hot(row, idx, float(r))
        o_ref[r:r + 256, :] = jnp.dot(hot, rows_ref[...], preferred_element_type=F32).astype(BF)


def select(parts, owners, capacity):
    unit = 4 * capacity
    return pl.pallas_call(
        functools.partial(select_kernel, capacity, unit),
        out_shape=jax.ShapeDtypeStruct((owners * unit, WIDE), BF),
        scratch_shapes=[pltpu.VMEM((2 * (parts.shape[1] - TABLE), WIDE), BF)],
        compiler_params=params(16),
        cost_estimate=pl.CostEstimate(flops=10**9, bytes_accessed=4 * 2**20, transcendentals=0),
        name="pick",
    )(parts)


def project_kernel(unit, padded, at_ref, c0_ref, c1_ref, c2_ref, c3_ref, c4_ref, near_ref, other_ref, pred_ref, ctxt_ref, w_ref, ctx,
                   raw, rows):
    count = near_ref.shape[0] // padded
    raw[:count] = near_ref[...].astype(F32).reshape(count, padded, WIDE)
    raw[count:] = other_ref[...].astype(F32).reshape(count, padded, WIDE)
    z, y, c = at_ref[0], at_ref[1], at_ref[2]
    row = 0
    for m in range(8):
        d = lax.rem(z - m + 8, 8)
        turn = (d % 2) * 4 + d // 2
        for n in range(4):
            for o in range(2):
                at = lax.rem(c + o, 2) * count + lax.rem(y - n + 4, 4) * 8 + turn
                rows[row:row + unit, :] = raw[at, :unit, :]
                row += unit
    w_ref[...] = rows[...].astype(BF)
    start = 0
    for c_ref in (c0_ref, c1_ref, c2_ref, c3_ref, c4_ref):
        ctx[start:start + c_ref.shape[0], :] = c_ref[...]
        start += c_ref.shape[0]
    for c in range(0, ctx.shape[1], 256):
        for r in range(0, ctx.shape[0], 256):
            ctxt_ref[c:c + 256, r:r + 256] = jnp.transpose(ctx[r:r + 256, c:c + 256].astype(F32)).astype(BF)
    pred_ref[...] = jnp.dot(ctx[...], w_ref[...], preferred_element_type=F32)


def project(at, pieces, near, other, unit, padded):
    quarter, width = pieces[0].shape
    vm = pl.BlockSpec(memory_space=pltpu.VMEM)
    return pl.pallas_call(
        functools.partial(project_kernel, unit, padded),
        in_specs=[pl.BlockSpec(memory_space=pltpu.SMEM)] + [vm] * 7,
        out_shape=[
            jax.ShapeDtypeStruct((4 * quarter, WIDE), F32),
            jax.ShapeDtypeStruct((width, 4 * quarter), BF),
            jax.ShapeDtypeStruct((width, WIDE), BF),
        ],
        scratch_shapes=[
            pltpu.VMEM((4 * quarter, width), BF),
            pltpu.VMEM((width // unit, padded, WIDE), F32),
            pltpu.VMEM((width, WIDE), F32),
        ],
        compiler_params=params(60),
        cost_estimate=pl.CostEstimate(flops=10**9, bytes_accessed=8 * 2**20, transcendentals=0),
        name="project",
    )(at, *pieces, near, other)


def land_kernel(unit, place_ref, t_ref, arrived_ref, pred_ref, ctxt_ref, err_ref, other_ref, own_ref, blocks):
    rows = err_ref.shape[0]
    quarter = rows // 4
    block = WIDE - 64
    slot = jnp.transpose(arrived_ref[:, 256:].astype(F32))[64:65, :].astype(jnp.int32)
    base = jnp.bitwise_and(place_ref[0] + 4 - t_ref[...], 3) * quarter - 1
    dst = jnp.where(slot > 0, slot + base, -1).astype(F32)
    row = count_rows(dst.shape[1])
    valid = lax.broadcasted_iota(jnp.int32, (256, WIDE), 1) < block
    for r in range(0, rows, 256):
        hot = one_hot(row, dst, float(r))
        target = jnp.dot(hot, arrived_ref[...], preferred_element_type=F32)
        err_ref[r:r + 256, :] = jnp.where(valid, pred_ref[r:r + 256, :] - target, 0.0).astype(BF)
    n = ctxt_ref.shape[0] // (2 * unit)
    chunk = 4 * 2 * unit
    blocks[...] = jnp.zeros_like(blocks)
    for i in range(0, 2 * n, 8):
        term = jnp.dot(ctxt_ref[i * unit:i * unit + chunk, :], err_ref[...], preferred_element_type=F32)
        for j in range(8):
            blocks[j % 2, (i + j) // 2, :unit, :] = term[j * unit:(j + 1) * unit, :]
    core = place_ref[1]
    other_ref[...] = blocks[1 - core].reshape(other_ref.shape).astype(BF)
    own_ref[...] = blocks[core].reshape(own_ref.shape)


def land(place, kinds, arrived, pred, ctxt, unit, padded):
    rows = pred.shape[0]
    n = ctxt.shape[0] // (2 * unit)
    vm = pl.BlockSpec(memory_space=pltpu.VMEM)
    return pl.pallas_call(
        functools.partial(land_kernel, unit),
        in_specs=[pl.BlockSpec(memory_space=pltpu.SMEM), vm, vm, vm, vm],
        out_shape=[
            jax.ShapeDtypeStruct((rows, WIDE), BF),
            jax.ShapeDtypeStruct((n * padded, WIDE), BF),
            jax.ShapeDtypeStruct((n * padded, WIDE), F32),
        ],
        scratch_shapes=[pltpu.VMEM((2, n, padded, WIDE), F32)],
        compiler_params=params(24),
        cost_estimate=pl.CostEstimate(flops=2 * 10**9, bytes_accessed=8 * 2**20, transcendentals=0),
        name="land",
    )(place, kinds, arrived, pred, ctxt)


def grad_kernel(err_ref, w_ref, own_ref, left_ref, far_ref, right_ref):
    quarter = own_ref.shape[0]
    for k, ref in enumerate((own_ref, left_ref, far_ref, right_ref)):
        part = lax.dot_general(err_ref[k * quarter:(k + 1) * quarter, :], w_ref[...], NT, preferred_element_type=F32)
        ref[...] = part.astype(ref.dtype)


def grad_parts(err, weight):
    quarter = err.shape[0] // 4
    width = weight.shape[0]
    return pl.pallas_call(
        grad_kernel,
        out_shape=[jax.ShapeDtypeStruct((quarter, width), t) for t in (F32, BF, BF, BF)],
        compiler_params=params(16),
        cost_estimate=pl.CostEstimate(flops=10**9, bytes_accessed=4 * 2**20, transcendentals=0),
        name="grad",
    )(err, weight)


def after(value, *earlier):
    return lax.optimization_barrier((value,) + earlier)[0]


def go(a, k, axis="tensor"):
    return lax.ppermute(a, axis, ring(lax.axis_size(axis), k))


def add(a, b):
    return (a.astype(F32) + b.astype(F32)).astype(BF)


def pieces_x(a):
    return [a] + [go(a, k) for k in (1, 2, 3)]


def local(
    t_query, t_key, t_value, t_segments, teacher_map, send_owner, send_slot, s_query, s_key, s_value, s_segments, s_weight
):
    x = lax.axis_index("tensor")
    core = lax.axis_index("core")
    rows = send_owner.shape[0]
    width = s_weight.shape[1]
    n_z, n_y, n_c = (lax.axis_size(a) for a in DP)
    owners = n_z * n_y * n_c
    capacity = 2 * rows // owners
    block = width // 4
    unit = 4 * capacity
    place2 = jnp.stack([x, core]).astype(jnp.int32)
    xs = x.astype(jnp.int32).reshape(1)
    own_rows = s_weight.shape[0]
    padded = own_rows + -own_rows % 8

    parts, mine = teacher(xs, t_segments, send_owner, send_slot, s_weight, t_query, t_key, t_value, teacher_map)
    parts = lax.all_to_all(parts, "tensor", 0, 0, tiled=True)
    outgoing = select(parts, owners, capacity)

    far = jnp.concatenate([mine] + [go(mine, k, "z") for k in (2, 4, 6)])
    far = jnp.concatenate([far, go(far, 1, "z")])
    first = go(far, 1, "y")
    last = go(far, 3, "y")
    context = student(s_segments, s_query, s_key, after(s_value, mine))

    outgoing, far, first, last, context = lax.optimization_barrier((outgoing, far, first, last, context))
    arrived = lax.all_to_all(outgoing, DP, 0, 0, tiled=True)

    right = go(context, 1)
    left = go(context, 3)
    contexts = (context, right, go(right[:rows // 2], 1), go(left[rows // 2:], 3), left)
    half = far.shape[0] // 2
    near = jnp.concatenate([far, first, go(first[:half], 1, "y"), go(last[half:], 3, "y"), last])
    where = jnp.stack([lax.axis_index(a) for a in DP]).astype(jnp.int32)
    prediction, turned, weight = project(where, contexts, near, go(near, 1, "core"), own_rows, padded)

    kinds = np.array([[(r % unit) // capacity for r in range(owners * unit)]], np.int32)
    err, other, term = land(place2, jnp.asarray(kinds), arrived, prediction, turned, own_rows, padded)
    own, *parts = grad_parts(err, weight)

    other, parts = lax.optimization_barrier((go(other, 1, "core"), parts))
    term = add(term, other)
    terms = lax.all_to_all(term, ("z", "y"), 0, 0, tiled=True)
    terms = terms.reshape(n_z * n_y, padded, WIDE)[:, :own_rows, :block]
    summed = jnp.sum(terms.astype(F32), axis=0) * (1.0 / math.sqrt(4 * rows * owners))
    whole = jnp.stack(pieces_x(summed))
    order = lax.rem(x - jnp.arange(4) + 4, 4)
    grad_weight = jnp.transpose(jnp.take(whole, order, axis=0), (1, 0, 2)).reshape(own_rows, width)

    grad_context = own + sum(go(part, 4 - k).astype(F32) for k, part in enumerate(parts, 1))
    return (grad_context, grad_weight)


def solution(mesh):
    fine = Mesh(mesh.devices.reshape(8, 4, 2, 4), DP + ("tensor",))
    both = DP + ("tensor",)
    placed = (
        P(DP, "tensor"),
        P(DP, "tensor"),
        P(DP, "tensor"),
        P(DP, None),
        P("tensor", None),
        P(both),
        P(both),
        P(both, None),
        P(both, None),
        P(both, None),
        P(both, None),
        P(DP, None),
    )
    return jax.shard_map(
        local, mesh=fine, in_specs=placed, out_specs=(P(both, None), P(DP, None)), check_vma=False
    )
```
